32 devices in a mesh: crop: 2 (over y), row: 16 (over z, x, core).
Axes of the slice: x: 2, y: 2, z: 4, core: 2. Of those that a mesh axis runs over, the one named last changes fastest.
Arguments:
- pair: bfloat16 [256, 128, 128], P(('crop', 'row')), parts along dimension 0, may hold values from -6 to 6
- residue_mask: int32 [256], P('crop'), parts along dimension 0, may hold values 0 or 1
- tri_proj: bfloat16 [2, 128, 512], replicated, may hold values from -0.5 to 0.5
- gate_out: bfloat16 [2, 128, 128], replicated, may hold values from -0.5 to 0.5
- w_out: bfloat16 [2, 128, 128], replicated, may hold values from -0.5 to 0.5
- norm_gain: float32 [2, 2, 128], replicated, may hold values from 0.25 to 1.75
Outputs:
- pair_out: bfloat16 [256, 128, 128], P(('crop', 'row')), parts along dimension 0
The draws below stay inside these ranges and needn't reach their ends.
There are 2 independent parts, one for each index of `crop`. The reference program is written for one: setup_inputs(seed, part) draws one part's arguments, and reference() takes and returns one part's arrays. A program takes and returns all parts, laid end to end along the dimension named above; an argument that names none is the same for every part. Nothing has to cross between parts.
Inputs may be any that keep to these rules, and one draw needn't show every extreme that they name: `residue_mask`: 1 marks a valid residue, 0 a padded one.
All inputs are finite; a program needn't handle non-finite values.
Results may differ from the reference program's by a relative error of at most 0.012.
Values may be sent and summed in bfloat16 or wider, within the bound.
A program may use at most 64 MiB of HBM per device.

```python
import jax
import jax.numpy as jnp
from jax import lax

C = 128
NRES = 128


def place_ends(entries, stream_key, least, high):
    longest = entries.shape.index(max(entries.shape))
    spots = []
    for shift in (0, 1):
        where = [jax.random.randint(jax.random.fold_in(stream_key, axis), (), 0, length) for axis, length in enumerate(entries.shape)]
        where[longest] = (where[longest] + shift) % entries.shape[longest]
        spots.append(tuple(where))
    return entries.at[spots[0]].set(least).at[spots[1]].set(high)


def block_levels(rng, shape, shards, low, largest):
    level, own = 1.0, jax.random.fold_in(rng, 6)
    for axis_at, shards_of in shards:
        draws = jnp.exp(jax.random.uniform(jax.random.fold_in(own, axis_at), (shards_of,), jnp.float32, low / len(shards), largest / len(shards)))
        level = level * jnp.repeat(draws, shape[axis_at] // shards_of).reshape([-1 if axis == axis_at else 1 for axis in range(len(shape))])
    return level


def noise(rng, dims, scale, limit, split=(), kind=jnp.bfloat16):
    values = jax.random.normal(rng, dims, jnp.float32) * scale
    if len(split) > 0:
        values = block_levels(rng, dims, split, -0.22, 0.18) * values
    return jnp.clip(values, min=-limit, max=limit).astype(kind)


def setup_inputs(seed: int = 0, part: int = 0) -> dict:
    arg_keys = jax.random.split(jax.random.key(seed), 7)
    part_keys = jax.random.split(jax.random.fold_in(arg_keys[6], part), 7)
    pair = noise(part_keys[0], (NRES, NRES, C), 1.0, 6.0, ((0, 16),))
    residue_mask = place_ends((jax.random.randint(part_keys[1], (NRES,), 0, 8) < 7).astype(jnp.int32), jax.random.fold_in(part_keys[1], 1), 0, 1)
    tri_proj = noise(arg_keys[2], (2, C, 4 * C), C ** -0.5, 0.5)
    gate_out = noise(arg_keys[3], (2, C, C), C ** -0.5, 0.5)
    w_out = noise(arg_keys[4], (2, C, C), C ** -0.5, 0.5)
    norm_gain = jnp.clip(1.0 + 0.15 * jax.random.normal(arg_keys[5], (2, 2, C), jnp.float32), 0.25, 1.75)
    return {"pair": pair, "residue_mask": residue_mask, "tri_proj": tri_proj, "gate_out": gate_out, "w_out": w_out, "norm_gain": norm_gain}


def layer_norm(values, gain):
    centre = lax.optimization_barrier(jnp.mean(values, axis=-1, keepdims=True))
    spread = lax.optimization_barrier(jnp.mean(jnp.square(values - centre), axis=-1, keepdims=True))
    return (values - centre) * lax.rsqrt(spread + 1e-05) * gain

def tri_update(state, pair_mask, proj, gate_weight, out_weight, gain_in, gain_out, incoming):
    state_f = state.astype(jnp.float32)
    normed = layer_norm(state_f, gain_in).astype(jnp.bfloat16)
    blocks = normed.reshape(NRES // 16, 16, NRES, C)
    mask_blocks = pair_mask.reshape(NRES // 16, 16, NRES, 1)

    def edge_block(item):
        piece, mask_piece = item
        projected = jnp.dot(piece.reshape(-1, C), proj, preferred_element_type=jnp.float32).reshape(16, NRES, 4 * C)
        left = (mask_piece * jax.nn.sigmoid(projected[..., C:2 * C]) * projected[..., :C]).astype(jnp.bfloat16)
        right = (mask_piece * jax.nn.sigmoid(projected[..., 3 * C:]) * projected[..., 2 * C:3 * C]).astype(jnp.bfloat16)
        return (left, right)
    left, right = lax.map(edge_block, (blocks, mask_blocks))
    left = jnp.moveaxis(left.reshape(NRES, NRES, C), 2, 0)
    right = jnp.moveaxis(right.reshape(NRES, NRES, C), 2, 0)

    def channel_product(item):
        left_c, right_c = item
        if incoming:
            return jnp.dot(left_c.T, right_c, preferred_element_type=jnp.float32).astype(jnp.bfloat16)
        return jnp.dot(left_c, right_c.T, preferred_element_type=jnp.float32).astype(jnp.bfloat16)
    product = lax.map(channel_product, (left, right))
    product = jnp.moveaxis(product, 0, 2)
    product_norm = layer_norm(product.astype(jnp.float32), gain_out).astype(jnp.bfloat16)
    gate_values = jax.nn.sigmoid(jnp.dot(normed.reshape(-1, C), gate_weight, preferred_element_type=jnp.float32))
    update = gate_values * jnp.dot(product_norm.reshape(-1, C), out_weight, preferred_element_type=jnp.float32)
    return (state_f + update.reshape(NRES, NRES, C)).astype(jnp.bfloat16)

def reference(pair, residue_mask, tri_proj, gate_out, w_out, norm_gain):
    valid = residue_mask.astype(jnp.float32)
    pair_mask = valid[:, None] * valid[None, :]
    state = tri_update(pair, pair_mask, tri_proj[0], gate_out[0], w_out[0], norm_gain[0, 0], norm_gain[0, 1], False)
    state = tri_update(state, pair_mask, tri_proj[1], gate_out[1], w_out[1], norm_gain[1, 0], norm_gain[1, 1], True)
    return state
```

```python
import functools

import jax
import jax.numpy as jnp
from jax import lax
from jax.experimental import pallas as pl
from jax.experimental.pallas import tpu as pltpu
from jax.sharding import PartitionSpec as P

F32, BF16 = jnp.float32, jnp.bfloat16
LANES, SUBL = 128, 8


def layer_norm_lead(values, gain):
    centre = jnp.mean(values, axis=0, keepdims=True)
    spread = jnp.mean(jnp.square(values - centre), axis=0, keepdims=True)
    return (values - centre) * lax.rsqrt(spread + 1e-05) * gain[:, None, None]


def layer_norm_last(values, gain):
    centre = jnp.mean(values, axis=-1, keepdims=True)
    spread = jnp.mean(jnp.square(values - centre), axis=-1, keepdims=True)
    return (values - centre) * lax.rsqrt(spread + 1e-05) * gain


def tri_update(state, pair_mask, proj, gate_weight, out_weight, gain_in, gain_out, incoming):
    channels = state.shape[2]
    state_f = state.astype(F32)
    normed = layer_norm_last(state_f, gain_in).astype(BF16)
    projected = jnp.einsum("rnk,kc->crn", normed, proj, preferred_element_type=F32)
    left = (
        pair_mask * jax.nn.sigmoid(projected[channels : 2 * channels]) * projected[:channels]
    ).astype(BF16)
    right = (
        pair_mask
        * jax.nn.sigmoid(projected[3 * channels :])
        * projected[2 * channels : 3 * channels]
    ).astype(BF16)
    left_all = lax.all_to_all(left, "row", split_axis=0, concat_axis=1, tiled=True)
    right_all = lax.all_to_all(right, "row", split_axis=0, concat_axis=1, tiled=True)
    sums = "cki,ckj->cij" if incoming else "cik,cjk->cij"
    product = jnp.einsum(sums, left_all, right_all, preferred_element_type=F32)
    returned = lax.all_to_all(
        product.astype(BF16), "row", split_axis=1, concat_axis=0, tiled=True
    )
    product_norm = layer_norm_lead(returned.astype(F32), gain_out).astype(BF16)
    gate_values = jax.nn.sigmoid(
        jnp.einsum("rnk,kd->rnd", normed, gate_weight, preferred_element_type=F32)
    )
    update = gate_values * jnp.einsum(
        "crn,cd->rnd", product_norm, out_weight, preferred_element_type=F32
    )
    return (state_f + update).astype(BF16)


def general(pair, residue_mask, tri_proj, gate_out, w_out, norm_gain):
    row_count = pair.shape[0]
    start = lax.axis_index("row") * row_count
    valid = residue_mask.astype(F32)
    row_valid = lax.dynamic_slice_in_dim(valid, start, row_count)
    pair_mask = row_valid[:, None] * valid[None, :]
    state = pair
    for u in (0, 1):
        state = tri_update(
            state, pair_mask, tri_proj[u], gate_out[u], w_out[u],
            norm_gain[u, 0], norm_gain[u, 1], u == 1,
        )
    return state


def norm_lead(values, gain):
    centre = jnp.mean(values, axis=0, keepdims=True)
    moved = values - centre
    spread = jnp.mean(jnp.square(moved), axis=0, keepdims=True)
    return moved * lax.rsqrt(spread + 1e-05) * gain


def sigmoid(x):
    return 0.5 * jnp.tanh(0.5 * x) + 0.5


def far_first(ring):
    half = ring // 2
    order = [half]
    for step in range(1, half):
        order += [half - step, half + step]
    return order


def kernel(
    ring, rows,
    mask_s, mask_v, pair, proj, gate_w, out_w, gains,
    out,
    state, normed, gates, edge, prod,
    edge_send0, edge_send1, edge_recv0, edge_recv1,
    prod_send0, prod_send1, prod_recv0, prod_recv1,
    send_sem, recv_sem,
):
    me = lax.axis_index("row")
    chan = pair.shape[2]
    res = pair.shape[1]
    pairs = rows // 2
    order = far_first(ring)

    barrier = pltpu.get_barrier_semaphore()
    for o in order:
        pl.semaphore_signal(
            barrier, inc=1, device_id={"row": lax.rem(me + o, ring)},
            device_id_type=pl.DeviceIdType.MESH,
        )

    gains_t = gains[...].T
    valid = mask_v[...].astype(F32)

    def send(src, dst, o, phase):
        to = lax.rem(me + o, ring)
        pltpu.make_async_remote_copy(
            src_ref=src.at[to], dst_ref=dst.at[me],
            send_sem=send_sem.at[phase, to], recv_sem=recv_sem.at[phase, me],
            device_id={"row": to}, device_id_type=pl.DeviceIdType.MESH,
        ).start()

    def wait_recv(dst, o, phase):
        frm = lax.rem(me + o, ring)
        pltpu.make_async_remote_copy(
            src_ref=dst.at[frm], dst_ref=dst.at[frm],
            send_sem=send_sem.at[phase, frm], recv_sem=recv_sem.at[phase, frm],
            device_id={"row": frm}, device_id_type=pl.DeviceIdType.MESH,
        ).wait_recv()
        return frm

    def wait_send(src, o, phase):
        to = lax.rem(me + o, ring)
        pltpu.make_async_remote_copy(
            src_ref=src.at[to], dst_ref=src.at[to],
            send_sem=send_sem.at[phase, to], recv_sem=recv_sem.at[phase, to],
            device_id={"row": to}, device_id_type=pl.DeviceIdType.MESH,
        ).wait_send()

    def tiles(first, second):
        shape = (ring, SUBL, res)
        return jnp.concatenate([first.reshape(shape), second.reshape(shape)], axis=1)

    for p in range(pairs):
        for r in (0, 1):
            state[p, :, r * res : (r + 1) * res] = pair[2 * p + r].astype(F32).T

    for u in (0, 1):
        edge_send, edge_recv = ((edge_send0, edge_recv0), (edge_send1, edge_recv1))[u]
        prod_send, prod_recv = ((prod_send0, prod_recv0), (prod_send1, prod_recv1))[u]
        gain_in = gains_t[:, 2 * u : 2 * u + 1]
        gain_out = gains_t[:, 2 * u + 1 : 2 * u + 2]
        proj_t = proj[u].astype(F32).T.astype(BF16)

        for p in range(pairs):
            nb = norm_lead(state[p], gain_in).astype(BF16)
            normed[p] = nb
            projected = jnp.dot(proj_t, nb, preferred_element_type=F32)
            row_valid = [mask_s[me * rows + 2 * p + r].astype(F32) * valid for r in (0, 1)]
            both = jnp.concatenate(row_valid, axis=1)
            for side in (0, 1):
                at = 2 * side * chan
                value = projected[at : at + chan]
                gate = projected[at + chan : at + 2 * chan]
                block = value * sigmoid(gate) * both
                edge_send[:, side, p * 16 : (p + 1) * 16, :] = tiles(
                    block[:, :res], block[:, res:]
                ).astype(BF16)

        if u == 0:
            pl.semaphore_wait(barrier, ring - 1)
        for o in order:
            send(edge_send, edge_recv, o, 2 * u)

        gate_t = gate_w[u].astype(F32).T.astype(BF16)
        out_t = out_w[u].astype(F32).T.astype(BF16)
        for p in range(pairs):
            gates[p] = sigmoid(jnp.dot(gate_t, normed[p], preferred_element_type=F32))

        count = rows * SUBL
        for side in (0, 1):
            at = pl.multiple_of(me * count, count)
            edge[side, pl.ds(at, count), :] = edge_send[me, side].astype(F32)
        for o in reversed(order):
            frm = wait_recv(edge_recv, o, 2 * u)
            at = pl.multiple_of(frm * count, count)
            for side in (0, 1):
                edge[side, pl.ds(at, count), :] = edge_recv[frm, side].astype(F32)

        for c in range(SUBL):
            left = edge.at[0][pl.ds(c, res, stride=SUBL), :]
            right = edge.at[1][pl.ds(c, res, stride=SUBL), :].astype(BF16)
            if u == 1:
                product = jnp.dot(left.T.astype(BF16), right, preferred_element_type=F32)
            else:
                product = lax.dot_general(
                    left.astype(BF16), right, (((1,), (1,)), ((), ())),
                    preferred_element_type=F32,
                )
            prod[c * res : (c + 1) * res, :] = product

        def gather(to):
            for p in range(pairs):
                parts = [
                    prod[pl.ds(to * rows + 2 * p + r, SUBL, stride=res), :] for r in (0, 1)
                ]
                prod_send[to, p * 16 : (p + 1) * 16, :] = jnp.concatenate(
                    parts, axis=0
                ).astype(BF16)

        for o in order:
            gather(lax.rem(me + o, ring))
            send(prod_send, prod_recv, o, 2 * u + 1)
        gather(me)
        prod_recv[me] = prod_send[me]
        for o in reversed(order):
            wait_recv(prod_recv, o, 2 * u + 1)

        for p in range(pairs):
            got = prod_recv[:, p * 16 : (p + 1) * 16, :].astype(F32)
            for r in (0, 1):
                block = got[:, r * SUBL : (r + 1) * SUBL, :].reshape(chan, res)
                pn = norm_lead(block, gain_out).astype(BF16)
                lanes = slice(r * res, (r + 1) * res)
                update = jnp.dot(out_t, pn, preferred_element_type=F32)
                new = (state[p, :, lanes] + gates[p, :, lanes] * update).astype(BF16)
                if u == 0:
                    state[p, :, lanes] = new.astype(F32)
                else:
                    out[:, 2 * p + r, :] = new

    for u in (0, 1):
        for o in order:
            wait_send((edge_send0, edge_send1)[u], o, 2 * u)
            wait_send((prod_send0, prod_send1)[u], o, 2 * u + 1)


def fused(ring, pair, residue_mask, tri_proj, gate_out, w_out, norm_gain):
    rows, res, chan = pair.shape
    vmem = pl.BlockSpec(memory_space=pltpu.VMEM)
    count = rows * SUBL
    edges = pltpu.VMEM((ring, 2, count, res), BF16)
    products = pltpu.VMEM((ring, count, res), BF16)
    wide = (rows // 2, chan, 2 * res)
    out = pl.pallas_call(
        functools.partial(kernel, ring, rows),
        out_shape=jax.ShapeDtypeStruct((chan, rows, res), BF16),
        in_specs=[pl.BlockSpec(memory_space=pltpu.SMEM)] + [vmem] * 6,
        out_specs=vmem,
        scratch_shapes=[
            pltpu.VMEM(wide, F32),
            pltpu.VMEM(wide, BF16),
            pltpu.VMEM(wide, F32),
            pltpu.VMEM((2, ring * count, res), F32),
            pltpu.VMEM((SUBL * res, res), F32),
            edges, edges, edges, edges,
            products, products, products, products,
            pltpu.SemaphoreType.DMA((4, ring)),
            pltpu.SemaphoreType.DMA((4, ring)),
        ],
        compiler_params=pltpu.CompilerParams(
            collective_id=0, has_side_effects=True, vmem_limit_bytes=32 * 1024 * 1024
        ),
        name="triangle_updates",
    )(
        residue_mask, residue_mask.reshape(1, res), pair, tri_proj, gate_out, w_out,
        norm_gain.reshape(4, chan),
    )
    return jnp.moveaxis(out, 0, 2)


def on_device(ring, pair, *rest):
    rows, res, chan = pair.shape
    if chan == ring * SUBL and res == LANES and ring * rows == res and rows % 2 == 0:
        return fused(ring, pair, *rest)
    return general(pair, *rest)


def solution(mesh):
    placed = (P(("crop", "row"), None, None), P("crop"), P(), P(), P(), P())
    return jax.shard_map(
        functools.partial(on_device, mesh.shape["row"]),
        mesh=mesh,
        in_specs=placed,
        out_specs=P(("crop", "row"), None, None),
        check_vma=False,
    )
```

```python
import functools

import jax
import jax.numpy as jnp
from jax import lax
from jax.experimental import pallas as pl
from jax.experimental.pallas import tpu as pltpu
from jax.sharding import PartitionSpec as P

F32, BF16 = jnp.float32, jnp.bfloat16
LANES, SUBL = 128, 8


def layer_norm_lead(values, gain):
    centre = jnp.mean(values, axis=0, keepdims=True)
    spread = jnp.mean(jnp.square(values - centre), axis=0, keepdims=True)
    return (values - centre) * lax.rsqrt(spread + 1e-05) * gain[:, None, None]


def layer_norm_last(values, gain):
    centre = jnp.mean(values, axis=-1, keepdims=True)
    spread = jnp.mean(jnp.square(values - centre), axis=-1, keepdims=True)
    return (values - centre) * lax.rsqrt(spread + 1e-05) * gain


def tri_update(state, pair_mask, proj, gate_weight, out_weight, gain_in, gain_out, incoming):
    channels = state.shape[2]
    state_f = state.astype(F32)
    normed = layer_norm_last(state_f, gain_in).astype(BF16)
    projected = jnp.einsum("rnk,kc->crn", normed, proj, preferred_element_type=F32)
    left = (
        pair_mask * jax.nn.sigmoid(projected[channels : 2 * channels]) * projected[:channels]
    ).astype(BF16)
    right = (
        pair_mask
        * jax.nn.sigmoid(projected[3 * channels :])
        * projected[2 * channels : 3 * channels]
    ).astype(BF16)
    left_all = lax.all_to_all(left, "row", split_axis=0, concat_axis=1, tiled=True)
    right_all = lax.all_to_all(right, "row", split_axis=0, concat_axis=1, tiled=True)
    sums = "cki,ckj->cij" if incoming else "cik,cjk->cij"
    product = jnp.einsum(sums, left_all, right_all, preferred_element_type=F32)
    returned = lax.all_to_all(
        product.astype(BF16), "row", split_axis=1, concat_axis=0, tiled=True
    )
    product_norm = layer_norm_lead(returned.astype(F32), gain_out).astype(BF16)
    gate_values = jax.nn.sigmoid(
        jnp.einsum("rnk,kd->rnd", normed, gate_weight, preferred_element_type=F32)
    )
    update = gate_values * jnp.einsum(
        "crn,cd->rnd", product_norm, out_weight, preferred_element_type=F32
    )
    return (state_f + update).astype(BF16)


def general(pair, residue_mask, tri_proj, gate_out, w_out, norm_gain):
    row_count = pair.shape[0]
    start = lax.axis_index("row") * row_count
    valid = residue_mask.astype(F32)
    row_valid = lax.dynamic_slice_in_dim(valid, start, row_count)
    pair_mask = row_valid[:, None] * valid[None, :]
    state = pair
    for u in (0, 1):
        state = tri_update(
            state, pair_mask, tri_proj[u], gate_out[u], w_out[u],
            norm_gain[u, 0], norm_gain[u, 1], u == 1,
        )
    return state


def norm_lead(values, gain):
    centre = jnp.mean(values, axis=0, keepdims=True)
    moved = values - centre
    spread = jnp.mean(jnp.square(moved), axis=0, keepdims=True)
    return moved * lax.rsqrt(spread + 1e-05) * gain


def sigmoid(x):
    return 0.5 * jnp.tanh(0.5 * x) + 0.5


def far_first(ring):
    half = ring // 2
    order = [half]
    for step in range(1, half):
        order += [half - step, half + step]
    return order


CHUNKS = 2
RIGHT, LEFT, BACK, EDGE, DONE = range(5)


def kernel(
    ring, rows,
    mask_h, pair_h, proj_h, gate_h, out_h, gains_h,
    out,
    mask_v, pair, proj, gate_w, out_w, gains,
    state, normed, gates,
    right_f, left_f, right_b, prod0, edge_f, prod1,
    right_send, right_recv, left_send, left_recv, back_send, back_recv,
    edge_send, edge_recv, done_send, done_recv,
    load_sem, send_sem, recv_sem,
):
    me = lax.axis_index("row")
    chan = pair.shape[2]
    res = pair.shape[1]
    half = ring // 2
    group = chan // half
    place = lax.rem(me, half)
    base = me - place
    per = rows // CHUNKS
    duos = per // 2
    everyone = far_first(ring)
    nearby = far_first(half)

    loads = [
        pltpu.make_async_copy(src, dst, load_sem.at[at])
        for at, (src, dst) in enumerate(
            ((pair_h, pair), (gains_h, gains), (proj_h, proj), (mask_h, mask_v),
             (gate_h, gate_w), (out_h, out_w))
        )
    ]
    for load in loads:
        load.start()

    barrier = pltpu.get_barrier_semaphore()
    for o in everyone:
        pl.semaphore_signal(
            barrier, inc=1, device_id={"row": lax.rem(me + o, ring)},
            device_id_type=pl.DeviceIdType.MESH,
        )

    def copy(src, dst, to, kind, ch, frm):
        return pltpu.make_async_remote_copy(
            src_ref=src, dst_ref=dst,
            send_sem=send_sem.at[kind, ch, to], recv_sem=recv_sem.at[kind, ch, frm],
            device_id={"row": to}, device_id_type=pl.DeviceIdType.MESH,
        )

    def far(o):
        return lax.rem(me + o, ring)

    def near(o):
        return base + lax.rem(place + o, half)

    def slot(device):
        return lax.rem(device, half)

    span = per * group

    def part(ch):
        return pl.ds(ch * span, span)

    loads[0].wait()
    loads[1].wait()
    gains_t = gains[...].T
    for r in range(rows):
        state[r] = pair[r].astype(F32).T

    def norm_rows(ch, gain):
        for r in range(ch * per, (ch + 1) * per):
            lanes = slice((r - ch * per) * res, (r - ch * per + 1) * res)
            normed[ch, :, lanes] = norm_lead(state[r], gain).astype(BF16)

    def edges(ch, weights_t):
        both = jnp.dot(weights_t, normed[ch], preferred_element_type=F32)
        return both[:chan] * sigmoid(both[chan:])

    norm_rows(0, gains_t[:, 0:1])
    loads[2].wait()
    loads[3].wait()
    valid = mask_v[...].astype(F32)
    lane = lax.broadcasted_iota(jnp.int32, (rows, res), 1)
    own = lax.broadcasted_iota(jnp.int32, (rows, res), 0) + me * rows
    own_valid = jnp.sum(
        jnp.where(lane == own, jnp.broadcast_to(valid, (rows, res)), 0.0), axis=1, keepdims=True
    )
    pair_mask = own_valid * valid

    def masked(ch, block):
        return [
            block[:, k * res : (k + 1) * res] * pair_mask[ch * per + k : ch * per + k + 1, :]
            for k in range(per)
        ]

    proj_t = proj[0].astype(F32).T.astype(BF16)
    for side, buf in ((1, right_send), (0, left_send)):
        for ch in range(CHUNKS):
            if side == 1 and ch > 0:
                norm_rows(ch, gains_t[:, 0:1])
            block = masked(ch, edges(ch, proj_t[2 * side * chan : 2 * (side + 1) * chan]))
            for k in range(per):
                at = (ch * per + k) * group
                buf[:, at : at + group, :] = block[k].reshape(half, group, res).astype(BF16)
            if side == 1:
                if ch == 0:
                    pl.semaphore_wait(barrier, ring - 1)
                for o in everyone:
                    to = far(o)
                    copy(
                        right_send.at[slot(to), part(ch)], right_recv.at[me, part(ch)],
                        to, RIGHT, ch, me,
                    ).start()
            else:
                for o in nearby:
                    to = near(o)
                    copy(
                        left_send.at[slot(to), part(ch)], left_recv.at[place, part(ch)],
                        to, LEFT, ch, me,
                    ).start()

    loads[4].wait()
    loads[5].wait()
    gate_t = [gate_w[u].astype(F32).T.astype(BF16) for u in (0, 1)]
    out_t = [out_w[u].astype(F32).T.astype(BF16) for u in (0, 1)]
    for ch in range(CHUNKS):
        gates[ch] = sigmoid(jnp.dot(gate_t[0], normed[ch], preferred_element_type=F32))

    def hold_right(device, ch, values):
        at = pl.multiple_of(device * (rows * group) + ch * span, span)
        right_f[pl.ds(at, span), :] = values.astype(F32)

    def hold_left(where, ch, values):
        at = pl.multiple_of(ch * (half * span) + where * span, span)
        left_f[pl.ds(at, span), :] = values.astype(F32)

    for ch in range(CHUNKS):
        hold_right(me, ch, right_send[place, part(ch), :])
        hold_left(place, ch, left_send[place, part(ch), :])
    for ch in range(CHUNKS):
        for o in reversed(everyone):
            frm = far(o)
            landed = right_recv.at[frm, part(ch)]
            copy(landed, landed, frm, RIGHT, ch, frm).wait_recv()
            hold_right(frm, ch, right_recv[frm, part(ch), :])
    for c in range(group):
        right_b[c] = right_f[pl.ds(c, res, stride=group), :].astype(BF16)
    count = half * per
    for ch in range(CHUNKS):
        for o in reversed(nearby):
            frm = near(o)
            landed = left_recv.at[slot(frm), part(ch)]
            copy(landed, landed, frm, LEFT, ch, frm).wait_recv()
            hold_left(slot(frm), ch, left_recv[slot(frm), part(ch), :])
        for c in range(group):
            left = left_f[pl.ds(ch * half * span + c, count, stride=group), :].astype(BF16)
            prod0[ch, c * count : (c + 1) * count, :] = lax.dot_general(
                left, right_b[c], (((1,), (1,)), ((), ())), preferred_element_type=F32
            )

        def give(where):
            for k in range(per):
                at = (ch * per + k) * group
                rows_of = prod0.at[ch][pl.ds(where * per + k, group, stride=count), :]
                back_send[where, at : at + group, :] = rows_of.astype(BF16)

        for o in nearby:
            to = near(o)
            give(slot(to))
            copy(
                back_send.at[slot(to), part(ch)], back_recv.at[place, part(ch)],
                to, BACK, ch, me,
            ).start()
        give(place)
        back_recv[place, part(ch), :] = back_send[place, part(ch), :]

    proj_t = proj[1].astype(F32).T.astype(BF16)
    size = per * SUBL
    for ch in range(CHUNKS):
        for o in reversed(nearby):
            frm = near(o)
            landed = back_recv.at[slot(frm), part(ch)]
            copy(landed, landed, frm, BACK, ch, frm).wait_recv()
        for k in range(per):
            r = ch * per + k
            got = back_recv[:, r * group : (r + 1) * group, :].reshape(chan, res)
            pn = norm_lead(got.astype(F32), gains_t[:, 1:2]).astype(BF16)
            update = jnp.dot(out_t[0], pn, preferred_element_type=F32)
            new = state[r] + gates[ch, :, k * res : (k + 1) * res] * update
            state[r] = new.astype(BF16).astype(F32)
        norm_rows(ch, gains_t[:, 2:3])
        for side in (0, 1):
            block = masked(ch, edges(ch, proj_t[2 * side * chan : 2 * (side + 1) * chan]))
            for d in range(duos):
                shape = (ring, SUBL, res)
                at = side * size + d * 16
                edge_send[ch, :, at : at + 16, :] = jnp.concatenate(
                    [block[2 * d].reshape(shape), block[2 * d + 1].reshape(shape)], axis=1
                ).astype(BF16)
        for o in everyone:
            to = far(o)
            copy(edge_send.at[ch, to], edge_recv.at[ch, me], to, EDGE, ch, me).start()

    for ch in range(CHUNKS):
        gates[ch] = sigmoid(jnp.dot(gate_t[1], normed[ch], preferred_element_type=F32))

    def hold_edges(device, ch, values):
        at = pl.multiple_of((ch * ring + device) * size, size)
        for side in (0, 1):
            edge_f[side, pl.ds(at, size), :] = values[side * size : (side + 1) * size].astype(F32)

    for ch in range(CHUNKS):
        hold_edges(me, ch, edge_send[ch, me])
        for o in reversed(everyone):
            frm = far(o)
            landed = edge_recv.at[ch, frm]
            copy(landed, landed, frm, EDGE, ch, frm).wait_recv()
            hold_edges(frm, ch, edge_recv[ch, frm])
    for c in range(SUBL):
        left = edge_f.at[0][pl.ds(c, res, stride=SUBL), :].T.astype(BF16)
        right = edge_f.at[1][pl.ds(c, res, stride=SUBL), :].astype(BF16)
        prod1[c * res : (c + 1) * res, :] = jnp.dot(left, right, preferred_element_type=F32)
    for ch in range(CHUNKS):

        def give_back(to):
            for d in range(duos):
                at = to * rows + ch * per + 2 * d
                parts = [prod1[pl.ds(at + k, SUBL, stride=res), :] for k in (0, 1)]
                done_send[ch, to, d * 16 : (d + 1) * 16, :] = jnp.concatenate(
                    parts, axis=0
                ).astype(BF16)

        for o in everyone:
            to = far(o)
            give_back(to)
            copy(done_send.at[ch, to], done_recv.at[ch, me], to, DONE, ch, me).start()
        give_back(me)
        done_recv[ch, me] = done_send[ch, me]

    for ch in range(CHUNKS):
        for o in reversed(everyone):
            frm = far(o)
            landed = done_recv.at[ch, frm]
            copy(landed, landed, frm, DONE, ch, frm).wait_recv()
        for d in range(duos):
            got = done_recv[ch, :, d * 16 : (d + 1) * 16, :].astype(F32)
            for j in (0, 1):
                k = 2 * d + j
                r = ch * per + k
                block = got[:, j * SUBL : (j + 1) * SUBL, :].reshape(chan, res)
                pn = norm_lead(block, gains_t[:, 3:4]).astype(BF16)
                update = jnp.dot(out_t[1], pn, preferred_element_type=F32)
                new = state[r] + gates[ch, :, k * res : (k + 1) * res] * update
                out[:, r, :] = new.astype(BF16)

    for ch in range(CHUNKS):
        for o in everyone:
            to = far(o)
            for kind, src in (
                (RIGHT, right_send.at[slot(to), part(ch)]),
                (EDGE, edge_send.at[ch, to]),
                (DONE, done_send.at[ch, to]),
            ):
                copy(src, src, to, kind, ch, to).wait_send()
        for o in nearby:
            to = near(o)
            for kind, src in (
                (LEFT, left_send.at[slot(to), part(ch)]),
                (BACK, back_send.at[slot(to), part(ch)]),
            ):
                copy(src, src, to, kind, ch, to).wait_send()


def fused(ring, pair, residue_mask, tri_proj, gate_out, w_out, norm_gain):
    rows, res, chan = pair.shape
    half = ring // 2
    group = chan // half
    per = rows // CHUNKS
    wide = (CHUNKS, chan, per * res)
    right_all = pltpu.VMEM((ring, rows * group, res), BF16)
    near_all = pltpu.VMEM((half, rows * group, res), BF16)
    edge_all = pltpu.VMEM((CHUNKS, ring, 2 * per * SUBL, res), BF16)
    done_all = pltpu.VMEM((CHUNKS, ring, per * SUBL, res), BF16)
    operands = (
        residue_mask.reshape(1, res), pair, tri_proj, gate_out, w_out, norm_gain.reshape(4, chan),
    )
    out = pl.pallas_call(
        functools.partial(kernel, ring, rows),
        out_shape=jax.ShapeDtypeStruct((chan, rows, res), BF16),
        in_specs=[pl.BlockSpec(memory_space=pl.ANY)] * 6,
        out_specs=pl.BlockSpec(memory_space=pltpu.VMEM),
        scratch_shapes=[pltpu.VMEM(x.shape, x.dtype) for x in operands]
        + [
            pltpu.VMEM((rows, chan, res), F32),
            pltpu.VMEM(wide, BF16),
            pltpu.VMEM(wide, F32),
            pltpu.VMEM((ring * rows * group, res), F32),
            pltpu.VMEM((half * rows * group, res), F32),
            pltpu.VMEM((group, res, res), BF16),
            pltpu.VMEM((CHUNKS, group * half * per, res), F32),
            pltpu.VMEM((2, ring * rows * SUBL, res), F32),
            pltpu.VMEM((SUBL * res, res), F32),
            near_all, right_all, near_all, near_all, near_all, near_all,
            edge_all, edge_all, done_all, done_all,
            pltpu.SemaphoreType.DMA((6,)),
            pltpu.SemaphoreType.DMA((5, CHUNKS, ring)),
            pltpu.SemaphoreType.DMA((5, CHUNKS, ring)),
        ],
        compiler_params=pltpu.CompilerParams(
            collective_id=0, has_side_effects=True, vmem_limit_bytes=40 * 1024 * 1024
        ),
        name="triangle_updates",
    )(*operands)
    return jnp.moveaxis(out, 0, 2)


def on_device(ring, pair, *rest):
    rows, res, chan = pair.shape
    fits = chan == ring * SUBL and res == LANES and ring * rows == res
    if fits and rows % (2 * CHUNKS) == 0 and ring % 2 == 0:
        return fused(ring, pair, *rest)
    return general(pair, *rest)


def solution(mesh):
    placed = (P(("crop", "row"), None, None), P("crop"), P(), P(), P(), P())
    return jax.shard_map(
        functools.partial(on_device, mesh.shape["row"]),
        mesh=mesh,
        in_specs=placed,
        out_specs=P(("crop", "row"), None, None),
        check_vma=False,
    )
```

```python
import functools

import jax
import jax.numpy as jnp
from jax import lax
from jax.experimental import pallas as pl
from jax.experimental.pallas import tpu as pltpu
from jax.sharding import PartitionSpec as P

F32, BF16 = jnp.float32, jnp.bfloat16
LANES, SUBL = 128, 8


def layer_norm_lead(values, gain):
    centre = jnp.mean(values, axis=0, keepdims=True)
    spread = jnp.mean(jnp.square(values - centre), axis=0, keepdims=True)
    return (values - centre) * lax.rsqrt(spread + 1e-05) * gain[:, None, None]


def layer_norm_last(values, gain):
    centre = jnp.mean(values, axis=-1, keepdims=True)
    spread = jnp.mean(jnp.square(values - centre), axis=-1, keepdims=True)
    return (values - centre) * lax.rsqrt(spread + 1e-05) * gain


def tri_update(state, pair_mask, proj, gate_weight, out_weight, gain_in, gain_out, incoming):
    channels = state.shape[2]
    state_f = state.astype(F32)
    normed = layer_norm_last(state_f, gain_in).astype(BF16)
    projected = jnp.einsum("rnk,kc->crn", normed, proj, preferred_element_type=F32)
    left = (
        pair_mask * jax.nn.sigmoid(projected[channels : 2 * channels]) * projected[:channels]
    ).astype(BF16)
    right = (
        pair_mask
        * jax.nn.sigmoid(projected[3 * channels :])
        * projected[2 * channels : 3 * channels]
    ).astype(BF16)
    left_all = lax.all_to_all(left, "row", split_axis=0, concat_axis=1, tiled=True)
    right_all = lax.all_to_all(right, "row", split_axis=0, concat_axis=1, tiled=True)
    sums = "cki,ckj->cij" if incoming else "cik,cjk->cij"
    product = jnp.einsum(sums, left_all, right_all, preferred_element_type=F32)
    returned = lax.all_to_all(
        product.astype(BF16), "row", split_axis=1, concat_axis=0, tiled=True
    )
    product_norm = layer_norm_lead(returned.astype(F32), gain_out).astype(BF16)
    gate_values = jax.nn.sigmoid(
        jnp.einsum("rnk,kd->rnd", normed, gate_weight, preferred_element_type=F32)
    )
    update = gate_values * jnp.einsum(
        "crn,cd->rnd", product_norm, out_weight, preferred_element_type=F32
    )
    return (state_f + update).astype(BF16)


def general(pair, residue_mask, tri_proj, gate_out, w_out, norm_gain):
    row_count = pair.shape[0]
    start = lax.axis_index("row") * row_count
    valid = residue_mask.astype(F32)
    row_valid = lax.dynamic_slice_in_dim(valid, start, row_count)
    pair_mask = row_valid[:, None] * valid[None, :]
    state = pair
    for u in (0, 1):
        state = tri_update(
            state, pair_mask, tri_proj[u], gate_out[u], w_out[u],
            norm_gain[u, 0], norm_gain[u, 1], u == 1,
        )
    return state


def norm_lead(values, gain):
    centre = jnp.mean(values, axis=0, keepdims=True)
    moved = values - centre
    spread = jnp.mean(jnp.square(moved), axis=0, keepdims=True)
    return moved * lax.rsqrt(spread + 1e-05) * gain


def sigmoid(x):
    return 0.5 * jnp.tanh(0.5 * x) + 0.5


def far_first(ring):
    half = ring // 2
    order = [half]
    for step in range(1, half):
        order += [half - step, half + step]
    return order


CHUNKS = 2
RIGHT, LEFT, BACK, EDGE, DONE = range(5)


def kernel(
    ring, rows,
    mask_h, pair_h, proj_h, gate_h, out_h, gains_h,
    out,
    mask_v, pair, proj, gate_w, out_w, gains,
    state, normed, gates,
    right_f, left_f, prod0, edge_f, prod1,
    right_send, right_recv, left_send, left_recv, back_send, back_recv,
    edge_send, edge_recv, done_send, done_recv,
    load_sem, send_sem, recv_sem,
):
    me = lax.axis_index("row")
    chan = pair.shape[2]
    res = pair.shape[1]
    half = ring // 2
    cuts = chan // half // SUBL
    place = lax.rem(me, half)
    base = me - place
    per = rows // CHUNKS
    duos = per // 2
    everyone = far_first(ring)
    nearby = far_first(half)

    loads = [
        pltpu.make_async_copy(src, dst, load_sem.at[at])
        for at, (src, dst) in enumerate(
            ((pair_h, pair), (gains_h, gains), (proj_h, proj), (mask_h, mask_v),
             (gate_h, gate_w), (out_h, out_w))
        )
    ]
    for load in loads:
        load.start()

    barrier = pltpu.get_barrier_semaphore()
    for o in everyone:
        pl.semaphore_signal(
            barrier, inc=1, device_id={"row": lax.rem(me + o, ring)},
            device_id_type=pl.DeviceIdType.MESH,
        )

    def copy(src, dst, to, kind, ch, frm):
        return pltpu.make_async_remote_copy(
            src_ref=src, dst_ref=dst,
            send_sem=send_sem.at[kind, ch, to], recv_sem=recv_sem.at[kind, ch, frm],
            device_id={"row": to}, device_id_type=pl.DeviceIdType.MESH,
        )

    def far(o):
        return lax.rem(me + o, ring)

    def near(o):
        return base + lax.rem(place + o, half)

    def slot(device):
        return lax.rem(device, half)

    span = per * SUBL

    def part(ch):
        return pl.ds(ch * span, span)

    loads[0].wait()
    loads[1].wait()
    gains_t = gains[...].T
    for r in range(rows):
        state[r] = pair[r].astype(F32).T

    def norm_rows(ch, gain):
        for r in range(ch * per, (ch + 1) * per):
            lanes = slice((r - ch * per) * res, (r - ch * per + 1) * res)
            normed[ch, :, lanes] = norm_lead(state[r], gain).astype(BF16)

    def edges(ch, weights_t):
        both = jnp.dot(weights_t, normed[ch], preferred_element_type=F32)
        return both[:chan] * sigmoid(both[chan:])

    norm_rows(0, gains_t[:, 0:1])
    loads[2].wait()
    loads[3].wait()
    valid = mask_v[...].astype(F32)
    lane = lax.broadcasted_iota(jnp.int32, (rows, res), 1)
    own = lax.broadcasted_iota(jnp.int32, (rows, res), 0) + me * rows
    own_valid = jnp.sum(
        jnp.where(lane == own, jnp.broadcast_to(valid, (rows, res)), 0.0), axis=1, keepdims=True
    )
    pair_mask = own_valid * valid

    def masked(ch, block):
        return [
            block[:, k * res : (k + 1) * res] * pair_mask[ch * per + k : ch * per + k + 1, :]
            for k in range(per)
        ]

    proj_t = proj[0].astype(F32).T.astype(BF16)
    for side, buf in ((1, right_send), (0, left_send)):
        for ch in range(CHUNKS):
            if side == 1 and ch > 0:
                norm_rows(ch, gains_t[:, 0:1])
            block = masked(ch, edges(ch, proj_t[2 * side * chan : 2 * (side + 1) * chan]))
            for d in range(duos):
                two = [block[2 * d + k].reshape(half, cuts, SUBL, res) for k in (0, 1)]
                at = ch * span + d * 16
                for cut in range(cuts):
                    buf[cut, :, at : at + 16, :] = jnp.concatenate(
                        [x[:, cut] for x in two], axis=1
                    ).astype(BF16)
            if side == 1:
                if ch == 0:
                    pl.semaphore_wait(barrier, ring - 1)
                for o in everyone:
                    to = far(o)
                    copy(
                        right_send.at[0, slot(to), part(ch)], right_recv.at[0, me, part(ch)],
                        to, RIGHT, ch, me,
                    ).start()
        if side == 0:
            for cut in range(cuts):
                for o in nearby:
                    to = near(o)
                    copy(
                        left_send.at[cut, slot(to)], left_recv.at[cut, place],
                        to, LEFT, cut, me,
                    ).start()
                if cut + 1 < cuts:
                    for o in everyone:
                        to = far(o)
                        copy(
                            right_send.at[cut + 1, slot(to)], right_recv.at[cut + 1, me],
                            to, RIGHT, CHUNKS + cut, me,
                        ).start()

    loads[4].wait()
    loads[5].wait()
    gate_t = [gate_w[u].astype(F32).T.astype(BF16) for u in (0, 1)]
    out_t = [out_w[u].astype(F32).T.astype(BF16) for u in (0, 1)]
    for ch in range(CHUNKS):
        gates[ch] = sigmoid(jnp.dot(gate_t[0], normed[ch], preferred_element_type=F32))

    block_rows = rows * SUBL
    count = half * rows
    for cut in range(cuts):
        at = pl.multiple_of(me * block_rows, block_rows)
        right_f[cut, pl.ds(at, block_rows), :] = right_send[cut, place].astype(F32)
        at = pl.multiple_of(place * block_rows, block_rows)
        left_f[cut, pl.ds(at, block_rows), :] = left_send[cut, place].astype(F32)

    def give(cut, where, ch):
        for d in range(ch * duos, (ch + 1) * duos):
            parts = [
                prod0.at[cut][pl.ds(where * rows + 2 * d + k, SUBL, stride=count), :]
                for k in (0, 1)
            ]
            back_send[cut, where, d * 16 : (d + 1) * 16, :] = jnp.concatenate(
                parts, axis=0
            ).astype(BF16)

    for cut in range(cuts):
        for o in reversed(everyone):
            frm = far(o)
            if cut == 0:
                for ch in range(CHUNKS):
                    landed = right_recv.at[0, frm, part(ch)]
                    copy(landed, landed, frm, RIGHT, ch, frm).wait_recv()
            else:
                landed = right_recv.at[cut, frm]
                copy(landed, landed, frm, RIGHT, CHUNKS + cut - 1, frm).wait_recv()
            at = pl.multiple_of(frm * block_rows, block_rows)
            right_f[cut, pl.ds(at, block_rows), :] = right_recv[cut, frm].astype(F32)
        for o in reversed(nearby):
            frm = near(o)
            landed = left_recv.at[cut, slot(frm)]
            copy(landed, landed, frm, LEFT, cut, frm).wait_recv()
            at = pl.multiple_of(slot(frm) * block_rows, block_rows)
            left_f[cut, pl.ds(at, block_rows), :] = left_recv[cut, slot(frm)].astype(F32)
        for c in range(SUBL):
            left = left_f.at[cut][pl.ds(c, count, stride=SUBL), :].astype(BF16)
            right = right_f.at[cut][pl.ds(c, res, stride=SUBL), :].astype(BF16)
            prod0[cut, c * count : (c + 1) * count, :] = lax.dot_general(
                left, right, (((1,), (1,)), ((), ())), preferred_element_type=F32
            )
        for ch in range(CHUNKS):
            for o in nearby:
                to = near(o)
                give(cut, slot(to), ch)
                copy(
                    back_send.at[cut, slot(to), part(ch)], back_recv.at[cut, place, part(ch)],
                    to, BACK, cut * CHUNKS + ch, me,
                ).start()
            give(cut, place, ch)
            back_recv[cut, place, part(ch), :] = back_send[cut, place, part(ch), :]

    proj_t = proj[1].astype(F32).T.astype(BF16)
    size = per * SUBL
    for ch in range(CHUNKS):
        for o in reversed(nearby):
            frm = near(o)
            for cut in range(cuts):
                landed = back_recv.at[cut, slot(frm), part(ch)]
                copy(landed, landed, frm, BACK, cut * CHUNKS + ch, frm).wait_recv()
        for k in range(per):
            r = ch * per + k
            tile = slice((r // 2) * 16, (r // 2 + 1) * 16)
            mine = slice((r % 2) * SUBL, (r % 2 + 1) * SUBL)
            got = jnp.stack(
                [back_recv[cut, :, tile, :].astype(F32)[:, mine] for cut in range(cuts)], axis=1
            ).reshape(chan, res)
            pn = norm_lead(got, gains_t[:, 1:2]).astype(BF16)
            update = jnp.dot(out_t[0], pn, preferred_element_type=F32)
            new = state[r] + gates[ch, :, k * res : (k + 1) * res] * update
            state[r] = new.astype(BF16).astype(F32)
        norm_rows(ch, gains_t[:, 2:3])
        for side in (0, 1):
            block = masked(ch, edges(ch, proj_t[2 * side * chan : 2 * (side + 1) * chan]))
            for d in range(duos):
                shape = (ring, SUBL, res)
                at = side * size + d * 16
                edge_send[ch, :, at : at + 16, :] = jnp.concatenate(
                    [block[2 * d].reshape(shape), block[2 * d + 1].reshape(shape)], axis=1
                ).astype(BF16)
        for o in everyone:
            to = far(o)
            copy(edge_send.at[ch, to], edge_recv.at[ch, me], to, EDGE, ch, me).start()

    for ch in range(CHUNKS):
        gates[ch] = sigmoid(jnp.dot(gate_t[1], normed[ch], preferred_element_type=F32))

    def hold_edges(device, ch, values):
        at = pl.multiple_of((ch * ring + device) * size, size)
        for side in (0, 1):
            edge_f[side, pl.ds(at, size), :] = values[side * size : (side + 1) * size].astype(F32)

    for ch in range(CHUNKS):
        hold_edges(me, ch, edge_send[ch, me])
        for o in reversed(everyone):
            frm = far(o)
            landed = edge_recv.at[ch, frm]
            copy(landed, landed, frm, EDGE, ch, frm).wait_recv()
            hold_edges(frm, ch, edge_recv[ch, frm])
    for c in range(SUBL):
        left = edge_f.at[0][pl.ds(c, res, stride=SUBL), :].T.astype(BF16)
        right = edge_f.at[1][pl.ds(c, res, stride=SUBL), :].astype(BF16)
        prod1[c * res : (c + 1) * res, :] = jnp.dot(left, right, preferred_element_type=F32)
    for ch in range(CHUNKS):

        def give_back(to):
            for d in range(duos):
                at = to * rows + ch * per + 2 * d
                parts = [prod1[pl.ds(at + k, SUBL, stride=res), :] for k in (0, 1)]
                done_send[ch, to, d * 16 : (d + 1) * 16, :] = jnp.concatenate(
                    parts, axis=0
                ).astype(BF16)

        for o in everyone:
            to = far(o)
            give_back(to)
            copy(done_send.at[ch, to], done_recv.at[ch, me], to, DONE, ch, me).start()
        give_back(me)
        done_recv[ch, me] = done_send[ch, me]

    for ch in range(CHUNKS):
        for o in reversed(everyone):
            frm = far(o)
            landed = done_recv.at[ch, frm]
            copy(landed, landed, frm, DONE, ch, frm).wait_recv()
        for d in range(duos):
            got = done_recv[ch, :, d * 16 : (d + 1) * 16, :].astype(F32)
            for j in (0, 1):
                k = 2 * d + j
                r = ch * per + k
                block = got[:, j * SUBL : (j + 1) * SUBL, :].reshape(chan, res)
                pn = norm_lead(block, gains_t[:, 3:4]).astype(BF16)
                update = jnp.dot(out_t[1], pn, preferred_element_type=F32)
                new = state[r] + gates[ch, :, k * res : (k + 1) * res] * update
                out[:, r, :] = new.astype(BF16)

    for o in everyone:
        to = far(o)
        sent = [(RIGHT, ch, right_send.at[0, slot(to), part(ch)]) for ch in range(CHUNKS)]
        sent += [
            (RIGHT, CHUNKS + cut - 1, right_send.at[cut, slot(to)]) for cut in range(1, cuts)
        ]
        sent += [(EDGE, ch, edge_send.at[ch, to]) for ch in range(CHUNKS)]
        sent += [(DONE, ch, done_send.at[ch, to]) for ch in range(CHUNKS)]
        for kind, at, src in sent:
            copy(src, src, to, kind, at, to).wait_send()
    for o in nearby:
        to = near(o)
        for cut in range(cuts):
            src = left_send.at[cut, slot(to)]
            copy(src, src, to, LEFT, cut, to).wait_send()
            for ch in range(CHUNKS):
                src = back_send.at[cut, slot(to), part(ch)]
                copy(src, src, to, BACK, cut * CHUNKS + ch, to).wait_send()


def fused(ring, pair, residue_mask, tri_proj, gate_out, w_out, norm_gain):
    rows, res, chan = pair.shape
    half = ring // 2
    cuts = chan // half // SUBL
    per = rows // CHUNKS
    wide = (CHUNKS, chan, per * res)
    right_all = pltpu.VMEM((cuts, ring, rows * SUBL, res), BF16)
    near_all = pltpu.VMEM((cuts, half, rows * SUBL, res), BF16)
    edge_all = pltpu.VMEM((CHUNKS, ring, 2 * per * SUBL, res), BF16)
    done_all = pltpu.VMEM((CHUNKS, ring, per * SUBL, res), BF16)
    operands = (
        residue_mask.reshape(1, res), pair, tri_proj, gate_out, w_out, norm_gain.reshape(4, chan),
    )
    out = pl.pallas_call(
        functools.partial(kernel, ring, rows),
        out_shape=jax.ShapeDtypeStruct((chan, rows, res), BF16),
        in_specs=[pl.BlockSpec(memory_space=pltpu.HBM)] * 6,
        out_specs=pl.BlockSpec(memory_space=pltpu.VMEM),
        scratch_shapes=[pltpu.VMEM(x.shape, x.dtype) for x in operands]
        + [
            pltpu.VMEM((rows, chan, res), F32),
            pltpu.VMEM(wide, BF16),
            pltpu.VMEM(wide, F32),
            pltpu.VMEM((cuts, ring * rows * SUBL, res), F32),
            pltpu.VMEM((cuts, half * rows * SUBL, res), F32),
            pltpu.VMEM((cuts, SUBL * half * rows, res), F32),
            pltpu.VMEM((2, ring * rows * SUBL, res), F32),
            pltpu.VMEM((SUBL * res, res), F32),
            near_all, right_all, near_all, near_all, near_all, near_all,
            edge_all, edge_all, done_all, done_all,
            pltpu.SemaphoreType.DMA((6,)),
            pltpu.SemaphoreType.DMA((5, cuts * CHUNKS, ring)),
            pltpu.SemaphoreType.DMA((5, cuts * CHUNKS, ring)),
        ],
        compiler_params=pltpu.CompilerParams(
            collective_id=0, has_side_effects=True, vmem_limit_bytes=62 * 1024 * 1024
        ),
        name="triangle_updates",
    )(*operands)
    return jnp.moveaxis(out, 0, 2)


def on_device(ring, pair, *rest):
    rows, res, chan = pair.shape
    fits = chan == ring * SUBL and res == LANES and ring * rows == res
    if fits and rows % (2 * CHUNKS) == 0 and ring % 2 == 0:
        return fused(ring, pair, *rest)
    return general(pair, *rest)


def solution(mesh):
    placed = (P(("crop", "row"), None, None), P("crop"), P(), P(), P(), P())
    return jax.shard_map(
        functools.partial(on_device, mesh.shape["row"]),
        mesh=mesh,
        in_specs=placed,
        out_specs=P(("crop", "row"), None, None),
        check_vma=False,
    )
```

```python
import functools

import jax
import jax.numpy as jnp
from jax import lax
from jax.experimental import pallas as pl
from jax.experimental.pallas import tpu as pltpu
from jax.sharding import PartitionSpec as P

F32, BF16 = jnp.float32, jnp.bfloat16
LANES, SUBL = 128, 8


def layer_norm_lead(values, gain):
    centre = jnp.mean(values, axis=0, keepdims=True)
    spread = jnp.mean(jnp.square(values - centre), axis=0, keepdims=True)
    return (values - centre) * lax.rsqrt(spread + 1e-05) * gain[:, None, None]


def layer_norm_last(values, gain):
    centre = jnp.mean(values, axis=-1, keepdims=True)
    spread = jnp.mean(jnp.square(values - centre), axis=-1, keepdims=True)
    return (values - centre) * lax.rsqrt(spread + 1e-05) * gain


def tri_update(state, pair_mask, proj, gate_weight, out_weight, gain_in, gain_out, incoming):
    channels = state.shape[2]
    state_f = state.astype(F32)
    normed = layer_norm_last(state_f, gain_in).astype(BF16)
    projected = jnp.einsum("rnk,kc->crn", normed, proj, preferred_element_type=F32)
    left = (
        pair_mask * jax.nn.sigmoid(projected[channels : 2 * channels]) * projected[:channels]
    ).astype(BF16)
    right = (
        pair_mask
        * jax.nn.sigmoid(projected[3 * channels :])
        * projected[2 * channels : 3 * channels]
    ).astype(BF16)
    left_all = lax.all_to_all(left, "row", split_axis=0, concat_axis=1, tiled=True)
    right_all = lax.all_to_all(right, "row", split_axis=0, concat_axis=1, tiled=True)
    sums = "cki,ckj->cij" if incoming else "cik,cjk->cij"
    product = jnp.einsum(sums, left_all, right_all, preferred_element_type=F32)
    returned = lax.all_to_all(
        product.astype(BF16), "row", split_axis=1, concat_axis=0, tiled=True
    )
    product_norm = layer_norm_lead(returned.astype(F32), gain_out).astype(BF16)
    gate_values = jax.nn.sigmoid(
        jnp.einsum("rnk,kd->rnd", normed, gate_weight, preferred_element_type=F32)
    )
    update = gate_values * jnp.einsum(
        "crn,cd->rnd", product_norm, out_weight, preferred_element_type=F32
    )
    return (state_f + update).astype(BF16)


def general(pair, residue_mask, tri_proj, gate_out, w_out, norm_gain):
    row_count = pair.shape[0]
    start = lax.axis_index("row") * row_count
    valid = residue_mask.astype(F32)
    row_valid = lax.dynamic_slice_in_dim(valid, start, row_count)
    pair_mask = row_valid[:, None] * valid[None, :]
    state = pair
    for u in (0, 1):
        state = tri_update(
            state, pair_mask, tri_proj[u], gate_out[u], w_out[u],
            norm_gain[u, 0], norm_gain[u, 1], u == 1,
        )
    return state


def norm_lead(values, gain):
    centre = jnp.mean(values, axis=0, keepdims=True)
    moved = values - centre
    spread = jnp.mean(jnp.square(moved), axis=0, keepdims=True)
    return moved * lax.rsqrt(spread + 1e-05) * gain


def sigmoid(x):
    return 0.5 * jnp.tanh(0.5 * x) + 0.5


def far_first(ring):
    half = ring // 2
    order = [half]
    for step in range(1, half):
        order += [half - step, half + step]
    return order


CHUNKS = 2
RIGHT, LEFT, BACK, EDGE, DONE = range(5)


def kernel(
    ring, rows,
    mask_h, pair_h, proj_h, gate_h, out_h, gains_h,
    out,
    mask_v, pair, proj, gate_w, out_w, gains,
    state, normed, gates,
    right_f, left_f, prod0, edge_f, prod1,
    right_send, right_recv, left_send, left_recv, back_send, back_recv,
    edge_send, edge_recv, done_send, done_recv,
    load_sem, send_sem, recv_sem,
):
    me = lax.axis_index("row")
    chan = pair.shape[2]
    res = pair.shape[1]
    half = ring // 2
    cuts = chan // half // SUBL
    place = lax.rem(me, half)
    base = me - place
    per = rows // CHUNKS
    duos = per // 2
    everyone = far_first(ring)
    nearby = far_first(half)

    loads = [
        pltpu.make_async_copy(src, dst, load_sem.at[at])
        for at, (src, dst) in enumerate(
            ((pair_h, pair), (gains_h, gains), (proj_h, proj), (mask_h, mask_v),
             (gate_h, gate_w), (out_h, out_w))
        )
    ]
    for load in loads:
        load.start()

    barrier = pltpu.get_barrier_semaphore()
    for o in everyone:
        pl.semaphore_signal(
            barrier, inc=1, device_id={"row": lax.rem(me + o, ring)},
            device_id_type=pl.DeviceIdType.MESH,
        )

    def copy(src, dst, to, kind, ch):
        return pltpu.make_async_remote_copy(
            src_ref=src, dst_ref=dst,
            send_sem=send_sem.at[kind, ch], recv_sem=recv_sem.at[kind, ch],
            device_id={"row": to}, device_id_type=pl.DeviceIdType.MESH,
        )

    def arrived(blocks, kind, ch):
        copy(blocks, blocks, far(1), kind, ch).wait_recv()

    def left_here(blocks, kind, ch):
        copy(blocks, blocks, far(1), kind, ch).wait_send()

    others, neighbours = pl.ds(0, ring - 1), pl.ds(0, half - 1)

    def far(o):
        return lax.rem(me + o, ring)

    def near(o):
        return base + lax.rem(place + o, half)

    def slot(device):
        return lax.rem(device, half)

    span = per * SUBL

    def part(ch):
        return pl.ds(ch * span, span)

    loads[0].wait()
    loads[1].wait()
    gains_t = gains[...].T
    for r in range(rows):
        state[r] = pair[r].astype(F32).T

    def norm_rows(ch, gain):
        for r in range(ch * per, (ch + 1) * per):
            lanes = slice((r - ch * per) * res, (r - ch * per + 1) * res)
            normed[ch, :, lanes] = norm_lead(state[r], gain).astype(BF16)

    def edges(ch, weights_t):
        both = jnp.dot(weights_t, normed[ch], preferred_element_type=F32)
        return both[:chan] * sigmoid(both[chan:])

    norm_rows(0, gains_t[:, 0:1])
    loads[2].wait()
    loads[3].wait()
    valid = mask_v[...].astype(F32)
    lane = lax.broadcasted_iota(jnp.int32, (rows, res), 1)
    own = lax.broadcasted_iota(jnp.int32, (rows, res), 0) + me * rows
    own_valid = jnp.sum(
        jnp.where(lane == own, jnp.broadcast_to(valid, (rows, res)), 0.0), axis=1, keepdims=True
    )
    pair_mask = own_valid * valid

    def masked(ch, block):
        return [
            block[:, k * res : (k + 1) * res] * pair_mask[ch * per + k : ch * per + k + 1, :]
            for k in range(per)
        ]

    proj_t = proj[0].astype(F32).T.astype(BF16)
    for side, buf in ((1, right_send), (0, left_send)):
        for ch in range(CHUNKS):
            if side == 1 and ch > 0:
                norm_rows(ch, gains_t[:, 0:1])
            block = masked(ch, edges(ch, proj_t[2 * side * chan : 2 * (side + 1) * chan]))
            for d in range(duos):
                two = [block[2 * d + k].reshape(half, cuts, SUBL, res) for k in (0, 1)]
                at = ch * span + d * 16
                for cut in range(cuts):
                    buf[cut, :, at : at + 16, :] = jnp.concatenate(
                        [x[:, cut] for x in two], axis=1
                    ).astype(BF16)
            if side == 1:
                if ch == 0:
                    pl.semaphore_wait(barrier, ring - 1)
                for o in everyone:
                    to = far(o)
                    copy(
                        right_send.at[0, slot(to), part(ch)], right_recv.at[0, me, part(ch)],
                        to, RIGHT, ch,
                    ).start()
        if side == 0:
            for cut in range(cuts):
                for o in nearby:
                    to = near(o)
                    copy(
                        left_send.at[cut, slot(to)], left_recv.at[cut, place],
                        to, LEFT, cut,
                    ).start()
                if cut + 1 < cuts:
                    for o in everyone:
                        to = far(o)
                        copy(
                            right_send.at[cut + 1, slot(to)], right_recv.at[cut + 1, me],
                            to, RIGHT, CHUNKS + cut,
                        ).start()

    loads[4].wait()
    loads[5].wait()
    gate_t = [gate_w[u].astype(F32).T.astype(BF16) for u in (0, 1)]
    out_t = [out_w[u].astype(F32).T.astype(BF16) for u in (0, 1)]
    for ch in range(CHUNKS):
        gates[ch] = sigmoid(jnp.dot(gate_t[0], normed[ch], preferred_element_type=F32))

    block_rows = rows * SUBL
    count = half * rows
    for cut in range(cuts):
        at = pl.multiple_of(me * block_rows, block_rows)
        right_f[cut, pl.ds(at, block_rows), :] = right_send[cut, place].astype(F32)
        at = pl.multiple_of(place * block_rows, block_rows)
        left_f[cut, pl.ds(at, block_rows), :] = left_send[cut, place].astype(F32)

    def give(cut, where, ch):
        for d in range(ch * duos, (ch + 1) * duos):
            parts = [
                prod0.at[cut][pl.ds(where * rows + 2 * d + k, SUBL, stride=count), :]
                for k in (0, 1)
            ]
            back_send[cut, where, d * 16 : (d + 1) * 16, :] = jnp.concatenate(
                parts, axis=0
            ).astype(BF16)

    for cut in range(cuts):
        if cut == 0:
            for ch in range(CHUNKS):
                arrived(right_recv.at[0, others, part(ch)], RIGHT, ch)
        else:
            arrived(right_recv.at[cut, others], RIGHT, CHUNKS + cut - 1)
        for o in reversed(everyone):
            frm = far(o)
            at = pl.multiple_of(frm * block_rows, block_rows)
            right_f[cut, pl.ds(at, block_rows), :] = right_recv[cut, frm].astype(F32)
        arrived(left_recv.at[cut, neighbours], LEFT, cut)
        for o in reversed(nearby):
            frm = near(o)
            at = pl.multiple_of(slot(frm) * block_rows, block_rows)
            left_f[cut, pl.ds(at, block_rows), :] = left_recv[cut, slot(frm)].astype(F32)
        for c in range(SUBL):
            left = left_f.at[cut][pl.ds(c, count, stride=SUBL), :].astype(BF16)
            right = right_f.at[cut][pl.ds(c, res, stride=SUBL), :].astype(BF16)
            prod0[cut, c * count : (c + 1) * count, :] = lax.dot_general(
                left, right, (((1,), (1,)), ((), ())), preferred_element_type=F32
            )
        for ch in range(CHUNKS):
            for o in nearby:
                to = near(o)
                give(cut, slot(to), ch)
                copy(
                    back_send.at[cut, slot(to), part(ch)], back_recv.at[cut, place, part(ch)],
                    to, BACK, cut * CHUNKS + ch,
                ).start()
            give(cut, place, ch)
            back_recv[cut, place, part(ch), :] = back_send[cut, place, part(ch), :]

    proj_t = proj[1].astype(F32).T.astype(BF16)
    size = per * SUBL
    for ch in range(CHUNKS):
        for cut in range(cuts):
            arrived(back_recv.at[cut, neighbours, part(ch)], BACK, cut * CHUNKS + ch)
        for k in range(per):
            r = ch * per + k
            tile = slice((r // 2) * 16, (r // 2 + 1) * 16)
            mine = slice((r % 2) * SUBL, (r % 2 + 1) * SUBL)
            got = jnp.stack(
                [back_recv[cut, :, tile, :].astype(F32)[:, mine] for cut in range(cuts)], axis=1
            ).reshape(chan, res)
            pn = norm_lead(got, gains_t[:, 1:2]).astype(BF16)
            update = jnp.dot(out_t[0], pn, preferred_element_type=F32)
            new = state[r] + gates[ch, :, k * res : (k + 1) * res] * update
            state[r] = new.astype(BF16).astype(F32)
        norm_rows(ch, gains_t[:, 2:3])
        for side in (0, 1):
            block = masked(ch, edges(ch, proj_t[2 * side * chan : 2 * (side + 1) * chan]))
            for d in range(duos):
                shape = (ring, SUBL, res)
                at = side * size + d * 16
                edge_send[ch, :, at : at + 16, :] = jnp.concatenate(
                    [block[2 * d].reshape(shape), block[2 * d + 1].reshape(shape)], axis=1
                ).astype(BF16)
        for o in everyone:
            to = far(o)
            copy(edge_send.at[ch, to], edge_recv.at[ch, me], to, EDGE, ch).start()

    for ch in range(CHUNKS):
        gates[ch] = sigmoid(jnp.dot(gate_t[1], normed[ch], preferred_element_type=F32))

    def hold_edges(device, ch, values):
        at = pl.multiple_of((ch * ring + device) * size, size)
        for side in (0, 1):
            edge_f[side, pl.ds(at, size), :] = values[side * size : (side + 1) * size].astype(F32)

    for ch in range(CHUNKS):
        hold_edges(me, ch, edge_send[ch, me])
        arrived(edge_recv.at[ch, others], EDGE, ch)
        for o in reversed(everyone):
            frm = far(o)
            hold_edges(frm, ch, edge_recv[ch, frm])
    for c in range(SUBL):
        left = edge_f.at[0][pl.ds(c, res, stride=SUBL), :].T.astype(BF16)
        right = edge_f.at[1][pl.ds(c, res, stride=SUBL), :].astype(BF16)
        prod1[c * res : (c + 1) * res, :] = jnp.dot(left, right, preferred_element_type=F32)
    for ch in range(CHUNKS):

        def give_back(to):
            for d in range(duos):
                at = to * rows + ch * per + 2 * d
                parts = [prod1[pl.ds(at + k, SUBL, stride=res), :] for k in (0, 1)]
                done_send[ch, to, d * 16 : (d + 1) * 16, :] = jnp.concatenate(
                    parts, axis=0
                ).astype(BF16)

        for o in everyone:
            to = far(o)
            give_back(to)
            copy(done_send.at[ch, to], done_recv.at[ch, me], to, DONE, ch).start()
        give_back(me)
        done_recv[ch, me] = done_send[ch, me]

    for ch in range(CHUNKS):
        arrived(done_recv.at[ch, others], DONE, ch)
        for d in range(duos):
            got = done_recv[ch, :, d * 16 : (d + 1) * 16, :].astype(F32)
            for j in (0, 1):
                k = 2 * d + j
                r = ch * per + k
                block = got[:, j * SUBL : (j + 1) * SUBL, :].reshape(chan, res)
                pn = norm_lead(block, gains_t[:, 3:4]).astype(BF16)
                update = jnp.dot(out_t[1], pn, preferred_element_type=F32)
                new = state[r] + gates[ch, :, k * res : (k + 1) * res] * update
                out[:, r, :] = new.astype(BF16)

    for ch in range(CHUNKS):
        left_here(right_recv.at[0, others, part(ch)], RIGHT, ch)
        left_here(edge_recv.at[ch, others], EDGE, ch)
        left_here(done_recv.at[ch, others], DONE, ch)
    for cut in range(cuts):
        if cut > 0:
            left_here(right_recv.at[cut, others], RIGHT, CHUNKS + cut - 1)
        left_here(left_recv.at[cut, neighbours], LEFT, cut)
        for ch in range(CHUNKS):
            left_here(back_recv.at[cut, neighbours, part(ch)], BACK, cut * CHUNKS + ch)


def fused(ring, pair, residue_mask, tri_proj, gate_out, w_out, norm_gain):
    rows, res, chan = pair.shape
    half = ring // 2
    cuts = chan // half // SUBL
    per = rows // CHUNKS
    wide = (CHUNKS, chan, per * res)
    right_all = pltpu.VMEM((cuts, ring, rows * SUBL, res), BF16)
    near_all = pltpu.VMEM((cuts, half, rows * SUBL, res), BF16)
    edge_all = pltpu.VMEM((CHUNKS, ring, 2 * per * SUBL, res), BF16)
    done_all = pltpu.VMEM((CHUNKS, ring, per * SUBL, res), BF16)
    operands = (
        residue_mask.reshape(1, res), pair, tri_proj, gate_out, w_out, norm_gain.reshape(4, chan),
    )
    out = pl.pallas_call(
        functools.partial(kernel, ring, rows),
        out_shape=jax.ShapeDtypeStruct((chan, rows, res), BF16),
        in_specs=[pl.BlockSpec(memory_space=pltpu.HBM)] * 6,
        out_specs=pl.BlockSpec(memory_space=pltpu.VMEM),
        scratch_shapes=[pltpu.VMEM(x.shape, x.dtype) for x in operands]
        + [
            pltpu.VMEM((rows, chan, res), F32),
            pltpu.VMEM(wide, BF16),
            pltpu.VMEM(wide, F32),
            pltpu.VMEM((cuts, ring * rows * SUBL, res), F32),
            pltpu.VMEM((cuts, half * rows * SUBL, res), F32),
            pltpu.VMEM((cuts, SUBL * half * rows, res), F32),
            pltpu.VMEM((2, ring * rows * SUBL, res), F32),
            pltpu.VMEM((SUBL * res, res), F32),
            near_all, right_all, near_all, near_all, near_all, near_all,
            edge_all, edge_all, done_all, done_all,
            pltpu.SemaphoreType.DMA((6,)),
            pltpu.SemaphoreType.DMA((5, cuts * CHUNKS)),
            pltpu.SemaphoreType.DMA((5, cuts * CHUNKS)),
        ],
        compiler_params=pltpu.CompilerParams(
            collective_id=0, has_side_effects=True, vmem_limit_bytes=62 * 1024 * 1024
        ),
        name="triangle_updates",
    )(*operands)
    return jnp.moveaxis(out, 0, 2)


def on_device(ring, pair, *rest):
    rows, res, chan = pair.shape
    fits = chan == ring * SUBL and res == LANES and ring * rows == res
    if fits and rows % (2 * CHUNKS) == 0 and ring % 2 == 0:
        return fused(ring, pair, *rest)
    return general(pair, *rest)


def solution(mesh):
    placed = (P(("crop", "row"), None, None), P("crop"), P(), P(), P(), P())
    return jax.shard_map(
        functools.partial(on_device, mesh.shape["row"]),
        mesh=mesh,
        in_specs=placed,
        out_specs=P(("crop", "row"), None, None),
        check_vma=False,
    )
```

```python
import functools

import jax
import jax.numpy as jnp
from jax import lax
from jax.experimental import pallas as pl
from jax.experimental.pallas import tpu as pltpu
from jax.sharding import PartitionSpec as P

F32, BF16 = jnp.float32, jnp.bfloat16
LANES, SUBL = 128, 8


def layer_norm_lead(values, gain):
    centre = jnp.mean(values, axis=0, keepdims=True)
    spread = jnp.mean(jnp.square(values - centre), axis=0, keepdims=True)
    return (values - centre) * lax.rsqrt(spread + 1e-05) * gain[:, None, None]


def layer_norm_last(values, gain):
    centre = jnp.mean(values, axis=-1, keepdims=True)
    spread = jnp.mean(jnp.square(values - centre), axis=-1, keepdims=True)
    return (values - centre) * lax.rsqrt(spread + 1e-05) * gain


def tri_update(state, pair_mask, proj, gate_weight, out_weight, gain_in, gain_out, incoming):
    channels = state.shape[2]
    state_f = state.astype(F32)
    normed = layer_norm_last(state_f, gain_in).astype(BF16)
    projected = jnp.einsum("rnk,kc->crn", normed, proj, preferred_element_type=F32)
    left = (
        pair_mask * jax.nn.sigmoid(projected[channels : 2 * channels]) * projected[:channels]
    ).astype(BF16)
    right = (
        pair_mask
        * jax.nn.sigmoid(projected[3 * channels :])
        * projected[2 * channels : 3 * channels]
    ).astype(BF16)
    left_all = lax.all_to_all(left, "row", split_axis=0, concat_axis=1, tiled=True)
    right_all = lax.all_to_all(right, "row", split_axis=0, concat_axis=1, tiled=True)
    sums = "cki,ckj->cij" if incoming else "cik,cjk->cij"
    product = jnp.einsum(sums, left_all, right_all, preferred_element_type=F32)
    returned = lax.all_to_all(
        product.astype(BF16), "row", split_axis=1, concat_axis=0, tiled=True
    )
    product_norm = layer_norm_lead(returned.astype(F32), gain_out).astype(BF16)
    gate_values = jax.nn.sigmoid(
        jnp.einsum("rnk,kd->rnd", normed, gate_weight, preferred_element_type=F32)
    )
    update = gate_values * jnp.einsum(
        "crn,cd->rnd", product_norm, out_weight, preferred_element_type=F32
    )
    return (state_f + update).astype(BF16)


def general(pair, residue_mask, tri_proj, gate_out, w_out, norm_gain):
    row_count = pair.shape[0]
    start = lax.axis_index("row") * row_count
    valid = residue_mask.astype(F32)
    row_valid = lax.dynamic_slice_in_dim(valid, start, row_count)
    pair_mask = row_valid[:, None] * valid[None, :]
    state = pair
    for u in (0, 1):
        state = tri_update(
            state, pair_mask, tri_proj[u], gate_out[u], w_out[u],
            norm_gain[u, 0], norm_gain[u, 1], u == 1,
        )
    return state


def norm_lead(values, gain):
    centre = jnp.mean(values, axis=0, keepdims=True)
    moved = values - centre
    spread = jnp.mean(jnp.square(moved), axis=0, keepdims=True)
    return moved * lax.rsqrt(spread + 1e-05) * gain


def sigmoid(x):
    return 0.5 * jnp.tanh(0.5 * x) + 0.5


def far_first(ring):
    half = ring // 2
    order = [half]
    for step in range(1, half):
        order += [half - step, half + step]
    return order


CHUNKS = 2
RIGHT, LEFT, BACK, EDGE, DONE = range(5)


def kernel(
    ring, rows,
    mask_h, pair_h, proj_h, gate_h, out_h, gains_h,
    out,
    mask_v, pair, proj, gate_w, out_w, gains,
    state, normed, gates,
    right_f, left_f, prod0, edge_f, prod1,
    right_send, right_recv, left_send, left_recv, back_send, back_recv,
    edge_send, edge_recv, done_send, done_recv,
    load_sem, send_sem, recv_sem,
):
    me = lax.axis_index("row")
    chan = pair.shape[2]
    res = pair.shape[1]
    half = ring // 2
    cuts = chan // half // SUBL
    place = lax.rem(me, half)
    base = me - place
    per = rows // CHUNKS
    duos = per // 2
    everyone = far_first(ring)
    nearby = far_first(half)

    loads = [
        pltpu.make_async_copy(src, dst, load_sem.at[at])
        for at, (src, dst) in enumerate(
            ((pair_h, pair), (gains_h, gains), (proj_h, proj), (mask_h, mask_v),
             (gate_h, gate_w), (out_h, out_w))
        )
    ]
    for load in loads:
        load.start()

    barrier = pltpu.get_barrier_semaphore()
    for o in everyone:
        pl.semaphore_signal(
            barrier, inc=1, device_id={"row": lax.rem(me + o, ring)},
            device_id_type=pl.DeviceIdType.MESH,
        )

    def copy(src, dst, to, kind, ch):
        return pltpu.make_async_remote_copy(
            src_ref=src, dst_ref=dst,
            send_sem=send_sem.at[kind, ch], recv_sem=recv_sem.at[kind, ch],
            device_id={"row": to}, device_id_type=pl.DeviceIdType.MESH,
        )

    def arrived(blocks, kind, ch):
        copy(blocks, blocks, far(1), kind, ch).wait_recv()

    def left_here(blocks, kind, ch):
        copy(blocks, blocks, far(1), kind, ch).wait_send()

    others, neighbours = pl.ds(0, ring - 1), pl.ds(0, half - 1)

    def far(o):
        return lax.rem(me + o, ring)

    def near(o):
        return base + lax.rem(place + o, half)

    def slot(device):
        return lax.rem(device, half)

    span = per * SUBL

    def part(ch):
        return pl.ds(ch * span, span)

    loads[0].wait()
    loads[1].wait()
    gains_t = gains[...].T
    for r in range(rows):
        state[r] = pair[r].astype(F32).T

    def norm_rows(ch, gain):
        for r in range(ch * per, (ch + 1) * per):
            lanes = slice((r - ch * per) * res, (r - ch * per + 1) * res)
            normed[ch, :, lanes] = norm_lead(state[r], gain).astype(BF16)

    def edges(ch, weights_t):
        both = jnp.dot(weights_t, normed[ch], preferred_element_type=F32)
        return both[:chan] * sigmoid(both[chan:])

    norm_rows(0, gains_t[:, 0:1])
    loads[2].wait()
    loads[3].wait()
    valid = mask_v[...].astype(F32)
    lane = lax.broadcasted_iota(jnp.int32, (rows, res), 1)
    own = lax.broadcasted_iota(jnp.int32, (rows, res), 0) + me * rows
    own_valid = jnp.sum(
        jnp.where(lane == own, jnp.broadcast_to(valid, (rows, res)), 0.0), axis=1, keepdims=True
    )
    pair_mask = own_valid * valid

    def masked(ch, block):
        return [
            block[:, k * res : (k + 1) * res] * pair_mask[ch * per + k : ch * per + k + 1, :]
            for k in range(per)
        ]

    proj_t = proj[0].astype(F32).T.astype(BF16)
    for side, buf in ((1, right_send), (0, left_send)):
        for ch in range(CHUNKS):
            if side == 1 and ch > 0:
                norm_rows(ch, gains_t[:, 0:1])
            block = masked(ch, edges(ch, proj_t[2 * side * chan : 2 * (side + 1) * chan]))
            for d in range(duos):
                two = [block[2 * d + k].reshape(half, cuts, SUBL, res) for k in (0, 1)]
                at = ch * span + d * 16
                for cut in range(cuts):
                    buf[cut, :, at : at + 16, :] = jnp.concatenate(
                        [x[:, cut] for x in two], axis=1
                    ).astype(BF16)
            if side == 1:
                if ch == 0:
                    pl.semaphore_wait(barrier, ring - 1)
                for o in everyone:
                    to = far(o)
                    copy(
                        right_send.at[0, slot(to), part(ch)], right_recv.at[0, me, part(ch)],
                        to, RIGHT, ch,
                    ).start()
        if side == 0:
            for cut in range(cuts):
                for o in nearby:
                    to = near(o)
                    copy(
                        left_send.at[cut, slot(to)], left_recv.at[cut, place],
                        to, LEFT, cut,
                    ).start()
                if cut + 1 < cuts:
                    for o in everyone:
                        to = far(o)
                        copy(
                            right_send.at[cut + 1, slot(to)], right_recv.at[cut + 1, me],
                            to, RIGHT, CHUNKS + cut,
                        ).start()

    loads[4].wait()
    loads[5].wait()
    gate_t = [gate_w[u].astype(F32).T.astype(BF16) for u in (0, 1)]
    out_t = [out_w[u].astype(F32).T.astype(BF16) for u in (0, 1)]
    for ch in range(CHUNKS):
        gates[ch] = sigmoid(jnp.dot(gate_t[0], normed[ch], preferred_element_type=F32))

    block_rows = rows * SUBL
    count = half * rows
    for cut in range(cuts):
        at = pl.multiple_of(me * block_rows, block_rows)
        right_f[cut, pl.ds(at, block_rows), :] = right_send[cut, place].astype(F32)
        at = pl.multiple_of(place * block_rows, block_rows)
        left_f[cut, pl.ds(at, block_rows), :] = left_send[cut, place].astype(F32)

    def give(cut, where, ch):
        for d in range(ch * duos, (ch + 1) * duos):
            parts = [
                prod0.at[cut][pl.ds(where * rows + 2 * d + k, SUBL, stride=count), :]
                for k in (0, 1)
            ]
            back_send[cut, where, d * 16 : (d + 1) * 16, :] = jnp.concatenate(
                parts, axis=0
            ).astype(BF16)

    for cut in range(cuts):
        if cut == 0:
            for ch in range(CHUNKS):
                arrived(right_recv.at[0, others, part(ch)], RIGHT, ch)
        else:
            arrived(right_recv.at[cut, others], RIGHT, CHUNKS + cut - 1)
        for o in reversed(everyone):
            frm = far(o)
            at = pl.multiple_of(frm * block_rows, block_rows)
            right_f[cut, pl.ds(at, block_rows), :] = right_recv[cut, frm].astype(F32)
        arrived(left_recv.at[cut, neighbours], LEFT, cut)
        for o in reversed(nearby):
            frm = near(o)
            at = pl.multiple_of(slot(frm) * block_rows, block_rows)
            left_f[cut, pl.ds(at, block_rows), :] = left_recv[cut, slot(frm)].astype(F32)
        for c in range(SUBL):
            left = left_f.at[cut][pl.ds(c, count, stride=SUBL), :].astype(BF16)
            right = right_f.at[cut][pl.ds(c, res, stride=SUBL), :].astype(BF16)
            prod0[cut, c * count : (c + 1) * count, :] = lax.dot_general(
                left, right, (((1,), (1,)), ((), ())), preferred_element_type=F32
            )
        for ch in range(CHUNKS):
            for o in nearby:
                to = near(o)
                give(cut, slot(to), ch)
                copy(
                    back_send.at[cut, slot(to), part(ch)], back_recv.at[cut, place, part(ch)],
                    to, BACK, cut * CHUNKS + ch,
                ).start()
            give(cut, place, ch)
            back_recv[cut, place, part(ch), :] = back_send[cut, place, part(ch), :]

    proj_t = proj[1].astype(F32).T.astype(BF16)
    size = per * SUBL
    for ch in range(CHUNKS):
        for cut in range(cuts):
            arrived(back_recv.at[cut, neighbours, part(ch)], BACK, cut * CHUNKS + ch)
        for k in range(per):
            r = ch * per + k
            tile = slice((r // 2) * 16, (r // 2 + 1) * 16)
            mine = slice((r % 2) * SUBL, (r % 2 + 1) * SUBL)
            got = jnp.stack(
                [back_recv[cut, :, tile, :].astype(F32)[:, mine] for cut in range(cuts)], axis=1
            ).reshape(chan, res)
            pn = norm_lead(got, gains_t[:, 1:2]).astype(BF16)
            update = jnp.dot(out_t[0], pn, preferred_element_type=F32)
            new = state[r] + gates[ch, :, k * res : (k + 1) * res] * update
            state[r] = new.astype(BF16).astype(F32)
        norm_rows(ch, gains_t[:, 2:3])
        for side in (0, 1):
            block = masked(ch, edges(ch, proj_t[2 * side * chan : 2 * (side + 1) * chan]))
            for d in range(duos):
                shape = (ring, SUBL, res)
                at = side * size + d * 16
                edge_send[ch, :, at : at + 16, :] = jnp.concatenate(
                    [block[2 * d].reshape(shape), block[2 * d + 1].reshape(shape)], axis=1
                ).astype(BF16)
        for o in everyone:
            to = far(o)
            copy(edge_send.at[ch, to], edge_recv.at[ch, me], to, EDGE, ch).start()

    for ch in range(CHUNKS):
        gates[ch] = sigmoid(jnp.dot(gate_t[1], normed[ch], preferred_element_type=F32))

    def hold_edges(device, ch, values):
        at = pl.multiple_of((ch * ring + device) * size, size)
        for side in (0, 1):
            edge_f[side, pl.ds(at, size), :] = values[side * size : (side + 1) * size].astype(F32)

    for ch in range(CHUNKS):
        hold_edges(me, ch, edge_send[ch, me])
        arrived(edge_recv.at[ch, others], EDGE, ch)
        for o in reversed(everyone):
            frm = far(o)
            hold_edges(frm, ch, edge_recv[ch, frm])
    for c in range(SUBL):
        left = edge_f.at[0][pl.ds(c, res, stride=SUBL), :].T.astype(BF16)
        right = edge_f.at[1][pl.ds(c, res, stride=SUBL), :].astype(BF16)
        prod1[c * res : (c + 1) * res, :] = jnp.dot(left, right, preferred_element_type=F32)
    for ch in range(CHUNKS):

        def give_back(to):
            for d in range(duos):
                at = to * rows + ch * per + 2 * d
                parts = [prod1[pl.ds(at + k, SUBL, stride=res), :] for k in (0, 1)]
                done_send[ch, to, d * 16 : (d + 1) * 16, :] = jnp.concatenate(
                    parts, axis=0
                ).astype(BF16)

        for o in everyone:
            to = far(o)
            give_back(to)
            copy(done_send.at[ch, to], done_recv.at[ch, me], to, DONE, ch).start()
        give_back(me)
        done_recv[ch, me] = done_send[ch, me]

    for ch in range(CHUNKS):
        arrived(done_recv.at[ch, others], DONE, ch)
        for d in range(duos):
            got = done_recv[ch, :, d * 16 : (d + 1) * 16, :].astype(F32)
            for j in (0, 1):
                k = 2 * d + j
                r = ch * per + k
                block = got[:, j * SUBL : (j + 1) * SUBL, :].reshape(chan, res)
                pn = norm_lead(block, gains_t[:, 3:4]).astype(BF16)
                update = jnp.dot(out_t[1], pn, preferred_element_type=F32)
                new = state[r] + gates[ch, :, k * res : (k + 1) * res] * update
                out[r] = new.T.astype(BF16)

    for ch in range(CHUNKS):
        left_here(right_recv.at[0, others, part(ch)], RIGHT, ch)
        left_here(edge_recv.at[ch, others], EDGE, ch)
        left_here(done_recv.at[ch, others], DONE, ch)
    for cut in range(cuts):
        if cut > 0:
            left_here(right_recv.at[cut, others], RIGHT, CHUNKS + cut - 1)
        left_here(left_recv.at[cut, neighbours], LEFT, cut)
        for ch in range(CHUNKS):
            left_here(back_recv.at[cut, neighbours, part(ch)], BACK, cut * CHUNKS + ch)


def fused(ring, pair, residue_mask, tri_proj, gate_out, w_out, norm_gain):
    rows, res, chan = pair.shape
    half = ring // 2
    cuts = chan // half // SUBL
    per = rows // CHUNKS
    wide = (CHUNKS, chan, per * res)
    right_all = pltpu.VMEM((cuts, ring, rows * SUBL, res), BF16)
    near_all = pltpu.VMEM((cuts, half, rows * SUBL, res), BF16)
    edge_all = pltpu.VMEM((CHUNKS, ring, 2 * per * SUBL, res), BF16)
    done_all = pltpu.VMEM((CHUNKS, ring, per * SUBL, res), BF16)
    operands = (
        residue_mask.reshape(1, res), pair, tri_proj, gate_out, w_out, norm_gain.reshape(4, chan),
    )
    return pl.pallas_call(
        functools.partial(kernel, ring, rows),
        out_shape=jax.ShapeDtypeStruct((rows, res, chan), BF16),
        in_specs=[pl.BlockSpec(memory_space=pltpu.HBM)] * 6,
        out_specs=pl.BlockSpec(memory_space=pltpu.VMEM),
        scratch_shapes=[pltpu.VMEM(x.shape, x.dtype) for x in operands]
        + [
            pltpu.VMEM((rows, chan, res), F32),
            pltpu.VMEM(wide, BF16),
            pltpu.VMEM(wide, F32),
            pltpu.VMEM((cuts, ring * rows * SUBL, res), F32),
            pltpu.VMEM((cuts, half * rows * SUBL, res), F32),
            pltpu.VMEM((cuts, SUBL * half * rows, res), F32),
            pltpu.VMEM((2, ring * rows * SUBL, res), F32),
            pltpu.VMEM((SUBL * res, res), F32),
            near_all, right_all, near_all, near_all, near_all, near_all,
            edge_all, edge_all, done_all, done_all,
            pltpu.SemaphoreType.DMA((6,)),
            pltpu.SemaphoreType.DMA((5, cuts * CHUNKS)),
            pltpu.SemaphoreType.DMA((5, cuts * CHUNKS)),
        ],
        compiler_params=pltpu.CompilerParams(
            collective_id=0, has_side_effects=True, vmem_limit_bytes=62 * 1024 * 1024
        ),
        name="triangle_updates",
    )(*operands)


def on_device(ring, pair, *rest):
    rows, res, chan = pair.shape
    fits = chan == ring * SUBL and res == LANES and ring * rows == res
    if fits and rows % (2 * CHUNKS) == 0 and ring % 2 == 0:
        return fused(ring, pair, *rest)
    return general(pair, *rest)


def solution(mesh):
    placed = (P(("crop", "row"), None, None), P("crop"), P(), P(), P(), P())
    return jax.shard_map(
        functools.partial(on_device, mesh.shape["row"]),
        mesh=mesh,
        in_specs=placed,
        out_specs=P(("crop", "row"), None, None),
        check_vma=False,
    )
```
